512 devices in a mesh: grp: 16 (over y, z_hi), par: 32 (over z_lo, x, core).
Axes of the slice: x: 4, y: 4, z: 16 (z_hi: 4, z_lo: 4; z = z_hi * 4 + z_lo), core: 2. Of those that a mesh axis runs over, the one named last changes fastest.
Arguments:
- particles: float32 [64, 1048576], P('grp', 'par'), may hold values from -6 to 6
- scores: float32 [64, 1048576], P('grp', 'par'), may hold values from -6 to 6
- kernel_width: float32 [1], replicated, may hold values from 1 to 4
Outputs:
- drive: float32 [64, 1048576], P('grp', 'par')
- repel: float32 [64, 1048576], P('grp', 'par')
The draws below stay inside these ranges and needn't reach their ends.
All inputs are finite; a program needn't handle non-finite values.
Results may differ from the reference program's by a relative error of at most 0.000092.
Values sent between devices are 32-bit elements; how exact they have to be, the bound alone decides.
A program may use at most 128 MiB of HBM per device.

```python
import math
import jax
import jax.numpy as jnp
from jax import lax

P_SIZE = 1048576
PARTICLES = 64


def draw_particles(key, part):
    key = jax.random.fold_in(key, 11)
    keys = jax.random.split(key, 4)
    center = jax.random.uniform(keys[0], (PARTICLES, 1), jnp.float32, -1.5, 1.5)
    spread = jax.random.uniform(keys[1], (PARTICLES, 1), jnp.float32, 0.3, 0.8)
    base = jax.random.normal(keys[2], (1, P_SIZE), jnp.float32)
    noise = jax.random.normal(keys[3], (PARTICLES, P_SIZE), jnp.float32)
    return jnp.clip(center * base + spread * noise, -6.0, 6.0)


def steps_of(key, shape, shards, low, top_value):
    def one(dim, shards_of):
        steps = jax.random.uniform(jax.random.fold_in(jax.random.fold_in(key, 6), dim), (shards_of,), jnp.float32, low / len(shards), top_value / len(shards))
        return jnp.repeat(jnp.exp(steps), shape[dim] // shards_of).reshape((-1,) + (1,) * (len(shape) - dim - 1))

    loudness = one(*shards[0])
    for cut in shards[1:]:
        loudness = loudness * one(*cut)
    return loudness


def centred(rng, dims, scale, limit, cuts=(), dtype=jnp.bfloat16):
    array = scale * jax.random.normal(rng, dims, jnp.float32)
    if cuts:
        array = array * steps_of(rng, dims, cuts, -0.22, 0.18)
    return jnp.clip(array, -limit, limit).astype(dtype)


def setup_inputs(seed: int = 0) -> dict:
    arg_keys = jax.random.split(jax.random.key(seed), 4)
    return {
        "particles": draw_particles(jax.random.fold_in(arg_keys[3], 71), 0),
        "scores": centred(arg_keys[1], (PARTICLES, P_SIZE), 1.0, 6.0, ((0, 16), (1, 32)), jnp.float32),
        "kernel_width": jnp.clip(jnp.exp(jax.random.uniform(arg_keys[2], (1,), jnp.float32, math.log(1.0), math.log(4.0))), 1.0, 4.0),
    }


def reference(particles, scores, kernel_width):
    highest = lax.Precision.HIGHEST
    norms = jnp.sum(particles * particles, axis=1)
    inner = lax.dot_general(particles, particles, (((1,), (1,)), ((), ())), precision=highest, preferred_element_type=jnp.float32)
    dist = norms[:, None] + norms[None, :] - 2.0 * inner
    kern = jnp.exp(-dist / (kernel_width[0] * P_SIZE))
    drive_sum = jnp.dot(kern, scores, precision=highest, preferred_element_type=jnp.float32)
    pull = jnp.dot(kern, particles, precision=highest, preferred_element_type=jnp.float32)
    weight = jnp.sum(kern, axis=1)
    drive = drive_sum / PARTICLES
    repel = (particles * weight[:, None] - pull) / (PARTICLES * kernel_width[0])
    return drive, repel
```

```python
import jax
import jax.numpy as jnp
from jax import lax
from jax.sharding import PartitionSpec as P

P_SIZE = 1048576
HIGHEST = lax.Precision.HIGHEST


def shards(particles, scores, kernel_width):
    width = kernel_width[0]
    groups = lax.axis_size("grp")
    count = particles.shape[0] * groups
    x = lax.all_to_all(particles, "grp", split_axis=1, concat_axis=0, tiled=True)
    s = lax.all_to_all(scores, "grp", split_axis=1, concat_axis=0, tiled=True)
    norms = jnp.sum(x * x, axis=1)
    inner = lax.dot_general(x, x, (((1,), (1,)), ((), ())), precision=HIGHEST, preferred_element_type=jnp.float32)
    dist = lax.psum(norms[:, None] + norms[None, :] - 2.0 * inner, ("grp", "par"))
    kern = jnp.exp(-dist / (width * P_SIZE))
    drive = jnp.dot(kern, s, precision=HIGHEST) / count
    pull = jnp.dot(kern, x, precision=HIGHEST)
    weight = jnp.sum(kern, axis=1)
    repel = (x * weight[:, None] - pull) / (count * width)
    drive = lax.all_to_all(drive, "grp", split_axis=0, concat_axis=1, tiled=True)
    repel = lax.all_to_all(repel, "grp", split_axis=0, concat_axis=1, tiled=True)
    return (drive, repel)


def solution(mesh):
    return jax.shard_map(
        shards,
        mesh=mesh,
        in_specs=(P("grp", "par"), P("grp", "par"), P()),
        out_specs=(P("grp", "par"), P("grp", "par")),
        check_vma=False,
    )
```

```python
import jax
import jax.numpy as jnp
from jax import lax
from jax.experimental import pallas as pl
from jax.experimental.pallas import tpu as pltpu
from jax.sharding import PartitionSpec as P

P_SIZE = 1048576
MESH = pl.DeviceIdType.MESH
HIGHEST = lax.Precision.HIGHEST
Y, ZH, ZL, X, C = 4, 4, 4, 4, 2
GROUPS, PLANE, LINE = Y * ZH, Y * X * C, ZH * ZL
EARLY = 1


def turn(a, b, n):
    return lax.rem(a + b, n)


def kernel(width_ref, x_ref, s_ref, repel_ref, drive_ref, xs, ss, pulls, drives, parts, scattered, lined, gathered,
           own, x_send, x_recv, s_send, s_recv, r_send, r_recv, d_send, d_recv,
           a_send, a_recv, b_send, b_recv, c_send, c_recv):
    g, p = lax.axis_index("grp"), lax.axis_index("par")
    y, zh = lax.div(g, ZH), lax.rem(g, ZH)
    zl, x, c = lax.div(p, X * C), lax.rem(lax.div(p, C), X), lax.rem(p, C)
    plane = (y * X + x) * C + c
    line = zh * ZL + zl
    rows, cols = xs.shape[1], xs.shape[2]

    def group_peer(k):
        return turn(y, lax.div(k, ZH), Y) * ZH + turn(zh, lax.rem(k, ZH), ZH)

    def plane_peer(k):
        py, px = turn(y, lax.div(k, X * C), Y), turn(x, lax.rem(lax.div(k, C), X), X)
        pc = turn(c, lax.rem(k, C), C)
        return (py * X + px) * C + pc, {"grp": py * ZH + zh, "par": zl * (X * C) + px * C + pc}

    def line_peer(k):
        ph, pz = turn(zh, lax.div(k, ZL), ZH), turn(zl, lax.rem(k, ZL), ZL)
        return {"grp": y * ZH + ph, "par": pz * (X * C) + x * C + c}

    def columns(q):
        return pl.ds(pl.multiple_of(q * cols, cols), cols)

    def each(low, high, body):
        lax.fori_loop(low, high, lambda k, _: (body(k), None)[1], None)

    barrier = pltpu.get_barrier_semaphore()

    def greet(where):
        pl.semaphore_signal(barrier, inc=1, device_id=where, device_id_type=MESH)

    each(1, GROUPS, lambda k: greet({"grp": group_peer(k)}))
    each(1, LINE, lambda k: greet(line_peer(k)))
    each(1, PLANE, lambda k: greet(plane_peer(k)[1]))
    pl.semaphore_wait(barrier, GROUPS + LINE + PLANE - 3)

    def bring(src, dst, send, recv):
        def copy(k):
            q = group_peer(k)
            return pltpu.make_async_remote_copy(
                src_ref=src.at[:, columns(q)], dst_ref=dst.at[g], send_sem=send.at[k], recv_sem=recv.at[k],
                device_id={"grp": q}, device_id_type=MESH)
        return copy

    def give(src, dst, send, recv):
        def copy(k):
            q = group_peer(k)
            return pltpu.make_async_remote_copy(
                src_ref=src.at[q], dst_ref=dst.at[:, columns(g)], send_sem=send.at[k], recv_sem=recv.at[k],
                device_id={"grp": q}, device_id_type=MESH)
        return copy

    x_in, s_in = bring(x_ref, xs, x_send, x_recv), bring(s_ref, ss, s_send, s_recv)
    r_out, d_out = give(pulls, repel_ref, r_send, r_recv), give(drives, drive_ref, d_send, d_recv)
    own_x = pltpu.make_async_copy(x_ref.at[:, columns(g)], xs.at[g], own.at[0])
    own_s = pltpu.make_async_copy(s_ref.at[:, columns(g)], ss.at[g], own.at[1])

    each(1, GROUPS, lambda k: x_in(k).start())
    own_x.start()
    own_s.start()
    each(1, ZH * EARLY, lambda k: s_in(k).start())

    own_x.wait()
    each(1, GROUPS, lambda k: x_in(k).wait_recv())
    block = xs[...].reshape(GROUPS * rows, cols)
    inner = lax.dot_general(block, block, (((1,), (1,)), ((), ())), precision=HIGHEST, preferred_element_type=jnp.float32)
    n = GROUPS * rows
    same = lax.broadcasted_iota(jnp.int32, (n, n), 0) == lax.broadcasted_iota(jnp.int32, (n, n), 1)
    norms = jnp.where(same, inner, 0.0)
    part = jnp.sum(norms, axis=1, keepdims=True) + jnp.sum(norms, axis=0, keepdims=True) - 2.0 * inner
    parts[...] = jnp.concatenate([part[: n // 2], part[n // 2 :]], axis=1).reshape(parts.shape)

    def scatter(k):
        q, where = plane_peer(k)
        return pltpu.make_async_remote_copy(
            src_ref=parts.at[q], dst_ref=scattered.at[plane], send_sem=a_send.at[k], recv_sem=a_recv.at[k],
            device_id=where, device_id_type=MESH)

    def along(k):
        return pltpu.make_async_remote_copy(
            src_ref=lined.at[line], dst_ref=lined.at[line], send_sem=b_send.at[k], recv_sem=b_recv.at[k],
            device_id=line_peer(k), device_id_type=MESH)

    def gather(k):
        return pltpu.make_async_remote_copy(
            src_ref=gathered.at[plane], dst_ref=gathered.at[plane], send_sem=c_send.at[k], recv_sem=c_recv.at[k],
            device_id=plane_peer(k)[1], device_id_type=MESH)

    each(1, PLANE, lambda k: scatter(k).start())
    scattered[plane] = parts[plane]
    each(1, PLANE, lambda k: scatter(k).wait_recv())
    lined[line] = jnp.sum(scattered[...], axis=0)
    each(1, LINE, lambda k: along(k).start())
    each(ZH * EARLY, GROUPS, lambda k: s_in(k).start())
    each(1, LINE, lambda k: along(k).wait_recv())
    gathered[plane] = jnp.sum(lined[...], axis=0)
    each(1, PLANE, lambda k: gather(k).start())
    each(1, PLANE, lambda k: gather(k).wait_recv())

    width = width_ref[0]
    both = gathered[...].reshape(n // 2, 2 * n)
    dist = jnp.concatenate([both[:, :n], both[:, n:]], axis=0)
    kern = jnp.exp(-dist / (width * P_SIZE))
    weight = jnp.sum(kern, axis=1, keepdims=True)
    block = xs[...].reshape(n, cols)
    pull = jnp.dot(kern, block, precision=HIGHEST, preferred_element_type=jnp.float32)
    pulls[...] = ((block * weight - pull) / (n * width)).reshape(pulls.shape)
    each(1, GROUPS, lambda k: r_out(k).start())
    own_r = pltpu.make_async_copy(pulls.at[g], repel_ref.at[:, columns(g)], own.at[2])
    own_r.start()

    own_s.wait()
    each(1, GROUPS, lambda k: s_in(k).wait_recv())
    block = ss[...].reshape(n, cols)
    drive = jnp.dot(kern, block, precision=HIGHEST, preferred_element_type=jnp.float32)
    drives[...] = (drive / n).reshape(drives.shape)
    each(1, GROUPS, lambda k: d_out(k).start())
    own_d = pltpu.make_async_copy(drives.at[g], drive_ref.at[:, columns(g)], own.at[3])
    own_d.start()

    each(1, GROUPS, lambda k: (x_in(k).wait_send(), s_in(k).wait_send()))
    each(1, PLANE, lambda k: (scatter(k).wait_send(), gather(k).wait_send()))
    each(1, LINE, lambda k: along(k).wait_send())
    own_r.wait()
    own_d.wait()
    each(1, GROUPS, lambda k: r_out(k).wait())
    each(1, GROUPS, lambda k: d_out(k).wait())


def shards(particles, scores, kernel_width):
    rows, length = particles.shape
    cols = length // GROUPS
    n = GROUPS * rows
    whole = pltpu.VMEM((GROUPS, rows, cols), jnp.float32)
    piece = n * n // PLANE
    out = jax.ShapeDtypeStruct(particles.shape, jnp.float32)
    dma = pltpu.SemaphoreType.DMA
    repel, drive = pl.pallas_call(
        kernel,
        out_shape=(out, out),
        in_specs=[pl.BlockSpec(memory_space=pltpu.SMEM)] + [pl.BlockSpec(memory_space=pl.ANY)] * 2,
        out_specs=(pl.BlockSpec(memory_space=pl.ANY),) * 2,
        scratch_shapes=[whole] * 4
        + [pltpu.VMEM((k, 1, piece), jnp.float32) for k in (PLANE, PLANE, LINE, PLANE)]
        + [dma((4,))] + [dma((GROUPS,))] * 8 + [dma((PLANE,))] * 2 + [dma((LINE,))] * 2 + [dma((PLANE,))] * 2,
        compiler_params=pltpu.CompilerParams(collective_id=0, has_side_effects=True, vmem_limit_bytes=24 << 20),
    )(kernel_width, particles, scores)
    return (drive, repel)


def solution(mesh):
    return jax.shard_map(
        shards,
        mesh=mesh,
        in_specs=(P("grp", "par"), P("grp", "par"), P()),
        out_specs=(P("grp", "par"), P("grp", "par")),
        check_vma=False,
    )
```

```python
import jax
import jax.numpy as jnp
from jax import lax
from jax.experimental import pallas as pl
from jax.experimental.pallas import tpu as pltpu
from jax.sharding import PartitionSpec as P

P_SIZE = 1048576
MESH = pl.DeviceIdType.MESH
HIGHEST = lax.Precision.HIGHEST
Y, ZH, ZL, X, C = 4, 4, 4, 4, 2
GROUPS, PLANE, LINE = Y * ZH, Y * X * C, ZH * ZL
EARLY = 1


def turn(a, b, n):
    return lax.rem(a + b, n)


def kernel(width_hbm, x_ref, s_ref, repel_ref, drive_ref, xs, ss, pulls, drives, parts, scattered, lined, gathered,
           width_ref, own, x_sem, s_sem, r_sem, d_sem, a_sem, b_sem, c_sem):
    g, p = lax.axis_index("grp"), lax.axis_index("par")
    y, zh = lax.div(g, ZH), lax.rem(g, ZH)
    zl, x, c = lax.div(p, X * C), lax.rem(lax.div(p, C), X), lax.rem(p, C)
    plane = (y * X + x) * C + c
    line = zh * ZL + zl
    rows, cols = xs.shape[1], xs.shape[2]

    def group_peer(k):
        return turn(y, lax.div(k, ZH), Y) * ZH + turn(zh, lax.rem(k, ZH), ZH)

    def plane_peer(k):
        py, px = turn(y, lax.div(k, X * C), Y), turn(x, lax.rem(lax.div(k, C), X), X)
        pc = turn(c, lax.rem(k, C), C)
        return (py * X + px) * C + pc, {"grp": py * ZH + zh, "par": zl * (X * C) + px * C + pc}

    def line_peer(k):
        ph, pz = turn(zh, lax.div(k, ZL), ZH), turn(zl, lax.rem(k, ZL), ZL)
        return {"grp": y * ZH + ph, "par": pz * (X * C) + x * C + c}

    def columns(q):
        return pl.ds(pl.multiple_of(q * cols, cols), cols)

    def each(low, high, body):
        lax.fori_loop(low, high, lambda k, _: (body(k), None)[1], None)

    barrier = pltpu.get_barrier_semaphore()

    def greet(where):
        pl.semaphore_signal(barrier, inc=1, device_id=where, device_id_type=MESH)

    each(1, GROUPS, lambda k: greet({"grp": group_peer(k)}))
    each(1, LINE, lambda k: greet(line_peer(k)))
    each(1, PLANE, lambda k: greet(plane_peer(k)[1]))
    pl.semaphore_wait(barrier, GROUPS + LINE + PLANE - 3)

    def bring(src, dst, sem):
        def copy(k):
            q = group_peer(k)
            return pltpu.make_async_remote_copy(
                src_ref=src.at[:, columns(q)], dst_ref=dst.at[g], send_sem=sem.at[0], recv_sem=sem.at[1],
                device_id={"grp": q}, device_id_type=MESH)
        return copy

    def give(src, dst, sem):
        def copy(k):
            q = group_peer(k)
            return pltpu.make_async_remote_copy(
                src_ref=src.at[q], dst_ref=dst.at[:, columns(g)], send_sem=sem.at[0], recv_sem=sem.at[1],
                device_id={"grp": q}, device_id_type=MESH)
        return copy

    def await_all(buffer, count, sem):
        whole = buffer.at[pl.ds(0, count)]
        pltpu.make_async_copy(whole, whole, sem).wait()

    x_in, s_in = bring(x_ref, xs, x_sem), bring(s_ref, ss, s_sem)
    r_out, d_out = give(pulls, repel_ref, r_sem), give(drives, drive_ref, d_sem)
    get_width = pltpu.make_async_copy(width_hbm, width_ref, own.at[4])
    own_x = pltpu.make_async_copy(x_ref.at[:, columns(g)], xs.at[g], own.at[0])
    own_s = pltpu.make_async_copy(s_ref.at[:, columns(g)], ss.at[g], own.at[1])

    each(1, GROUPS, lambda k: x_in(k).start())
    own_x.start()
    own_s.start()
    get_width.start()
    each(1, ZH * EARLY, lambda k: s_in(k).start())

    own_x.wait()
    await_all(xs, GROUPS - 1, x_sem.at[1])
    block = xs[...].reshape(GROUPS * rows, cols)
    inner = lax.dot_general(block, block, (((1,), (1,)), ((), ())), precision=HIGHEST, preferred_element_type=jnp.float32)
    n = GROUPS * rows
    same = lax.broadcasted_iota(jnp.int32, (n, n), 0) == lax.broadcasted_iota(jnp.int32, (n, n), 1)
    norms = jnp.where(same, inner, 0.0)
    part = jnp.sum(norms, axis=1, keepdims=True) + jnp.sum(norms, axis=0, keepdims=True) - 2.0 * inner
    parts[...] = jnp.concatenate([part[: n // 2], part[n // 2 :]], axis=1).reshape(parts.shape)

    def scatter(k):
        q, where = plane_peer(k)
        return pltpu.make_async_remote_copy(
            src_ref=parts.at[q], dst_ref=scattered.at[plane], send_sem=a_sem.at[0], recv_sem=a_sem.at[1],
            device_id=where, device_id_type=MESH)

    def along(k):
        return pltpu.make_async_remote_copy(
            src_ref=lined.at[line], dst_ref=lined.at[line], send_sem=b_sem.at[0], recv_sem=b_sem.at[1],
            device_id=line_peer(k), device_id_type=MESH)

    def gather(k):
        return pltpu.make_async_remote_copy(
            src_ref=gathered.at[plane], dst_ref=gathered.at[plane], send_sem=c_sem.at[0], recv_sem=c_sem.at[1],
            device_id=plane_peer(k)[1], device_id_type=MESH)

    each(1, PLANE, lambda k: scatter(k).start())
    scattered[plane] = parts[plane]
    await_all(scattered, PLANE - 1, a_sem.at[1])
    lined[line] = jnp.sum(scattered[...], axis=0)
    each(1, LINE, lambda k: along(k).start())
    each(ZH * EARLY, GROUPS, lambda k: s_in(k).start())
    await_all(lined, LINE - 1, b_sem.at[1])
    gathered[plane] = jnp.sum(lined[...], axis=0)
    each(1, PLANE, lambda k: gather(k).start())
    await_all(gathered, PLANE - 1, c_sem.at[1])

    get_width.wait()
    width = width_ref[0]
    both = gathered[...].reshape(n // 2, 2 * n)
    dist = jnp.concatenate([both[:, :n], both[:, n:]], axis=0)
    kern = jnp.exp(-dist / (width * P_SIZE))
    weight = jnp.sum(kern, axis=1, keepdims=True)
    block = xs[...].reshape(n, cols)
    pull = jnp.dot(kern, block, precision=HIGHEST, preferred_element_type=jnp.float32)
    pulls[...] = ((block * weight - pull) / (n * width)).reshape(pulls.shape)
    each(1, GROUPS, lambda k: r_out(k).start())
    own_r = pltpu.make_async_copy(pulls.at[g], repel_ref.at[:, columns(g)], own.at[2])
    own_r.start()

    own_s.wait()
    await_all(ss, GROUPS - 1, s_sem.at[1])
    block = ss[...].reshape(n, cols)
    drive = jnp.dot(kern, block, precision=HIGHEST, preferred_element_type=jnp.float32)
    drives[...] = (drive / n).reshape(drives.shape)
    each(1, GROUPS, lambda k: d_out(k).start())
    own_d = pltpu.make_async_copy(drives.at[g], drive_ref.at[:, columns(g)], own.at[3])
    own_d.start()

    await_all(xs, GROUPS - 1, x_sem.at[0])
    await_all(ss, GROUPS - 1, s_sem.at[0])
    await_all(parts, PLANE - 1, a_sem.at[0])
    await_all(lined, LINE - 1, b_sem.at[0])
    await_all(gathered, PLANE - 1, c_sem.at[0])
    own_r.wait()
    own_d.wait()
    for sem in (r_sem, d_sem):
        await_all(pulls, GROUPS - 1, sem.at[0])
        await_all(pulls, GROUPS - 1, sem.at[1])


def shards(particles, scores, kernel_width):
    rows, length = particles.shape
    cols = length // GROUPS
    n = GROUPS * rows
    whole = pltpu.VMEM((GROUPS, rows, cols), jnp.float32)
    piece = n * n // PLANE
    out = jax.ShapeDtypeStruct(particles.shape, jnp.float32)
    dma = pltpu.SemaphoreType.DMA
    repel, drive = pl.pallas_call(
        kernel,
        out_shape=(out, out),
        in_specs=[pl.BlockSpec(memory_space=pl.ANY)] * 3,
        out_specs=(pl.BlockSpec(memory_space=pltpu.VMEM),) * 2,
        scratch_shapes=[whole] * 4
        + [pltpu.VMEM((k, 1, piece), jnp.float32) for k in (PLANE, PLANE, LINE, PLANE)]
        + [pltpu.SMEM((1,), jnp.float32), dma((5,))] + [dma((2,))] * 7,
        compiler_params=pltpu.CompilerParams(collective_id=0, has_side_effects=True, vmem_limit_bytes=55050240),
    )(kernel_width, particles, scores)
    return (drive, repel)


def solution(mesh):
    return jax.shard_map(
        shards,
        mesh=mesh,
        in_specs=(P("grp", "par"), P("grp", "par"), P()),
        out_specs=(P("grp", "par"), P("grp", "par")),
        check_vma=False,
    )
```

```python
import jax
import jax.numpy as jnp
from jax import lax
from jax.experimental import pallas as pl
from jax.experimental.pallas import tpu as pltpu
from jax.sharding import PartitionSpec as P

P_SIZE = 1048576
MESH = pl.DeviceIdType.MESH
HIGHEST = lax.Precision.HIGHEST
Y, ZH, ZL, X, C = 4, 4, 4, 4, 2
GROUPS, PLANE, LINE, OWNERS = Y * ZH, Y * X * C, ZH * ZL, Y * X


def turn(a, b, n):
    return lax.rem(a + b, n)


def kernel(width_hbm, x_ref, s_ref, repel_ref, drive_ref, xs, ss, pulls, drives, parts, scattered, lined, gathered,
           width_ref, own, x_sem, s_sem, r_sem, d_sem, a_sem, b_sem, c_sem):
    g, p = lax.axis_index("grp"), lax.axis_index("par")
    y, zh = lax.div(g, ZH), lax.rem(g, ZH)
    zl, x, c = lax.div(p, X * C), lax.rem(lax.div(p, C), X), lax.rem(p, C)
    plane = (y * X + x) * C + c
    owner, line = y * X + x, zh * ZL + zl
    rows, cols = xs.shape[1], xs.shape[2]

    def group_peer(k):
        return turn(y, lax.div(k, ZH), Y) * ZH + turn(zh, lax.rem(k, ZH), ZH)

    def plane_peer(k):
        py, px = turn(y, lax.div(k, X * C), Y), turn(x, lax.rem(lax.div(k, C), X), X)
        pc = turn(c, lax.rem(k, C), C)
        return (py * X + px) * C + pc, {"grp": py * ZH + zh, "par": zl * (X * C) + px * C + pc}

    def owner_peer(k):
        py, px = turn(y, lax.div(k, X), Y), turn(x, lax.rem(k, X), X)
        return py * X + px, {"grp": py * ZH + zh, "par": zl * (X * C) + px * C}

    def line_peer(k):
        ph, pz = turn(zh, lax.div(k, ZL), ZH), turn(zl, lax.rem(k, ZL), ZL)
        return {"grp": y * ZH + ph, "par": pz * (X * C) + x * C + c}

    def columns(q):
        return pl.ds(pl.multiple_of(q * cols, cols), cols)

    def each(low, high, body):
        lax.fori_loop(low, high, lambda k, _: (body(k), None)[1], None)

    barrier = pltpu.get_barrier_semaphore()

    def greet(where):
        pl.semaphore_signal(barrier, inc=1, device_id=where, device_id_type=MESH)

    each(1, GROUPS, lambda k: greet({"grp": group_peer(k)}))

    @pl.when(c == 0)
    def _():
        each(1, LINE, lambda k: greet(line_peer(k)))
        each(1, PLANE, lambda k: greet(plane_peer(k)[1]))
        pl.semaphore_wait(barrier, GROUPS + LINE + PLANE - 3)

    @pl.when(c != 0)
    def _():
        each(0, OWNERS, lambda k: greet(owner_peer(k)[1]))
        pl.semaphore_wait(barrier, GROUPS + OWNERS - 1)

    def bring(src, dst, sem):
        def copy(k):
            q = group_peer(k)
            return pltpu.make_async_remote_copy(
                src_ref=src.at[:, columns(q)], dst_ref=dst.at[g], send_sem=sem.at[0], recv_sem=sem.at[1],
                device_id={"grp": q}, device_id_type=MESH)
        return copy

    def give(src, dst, sem):
        def copy(k):
            q = group_peer(k)
            return pltpu.make_async_remote_copy(
                src_ref=src.at[q], dst_ref=dst.at[:, columns(g)], send_sem=sem.at[0], recv_sem=sem.at[1],
                device_id={"grp": q}, device_id_type=MESH)
        return copy

    def await_all(buffer, count, sem):
        whole = buffer.at[pl.ds(0, count)]
        pltpu.make_async_copy(whole, whole, sem).wait()

    x_in, s_in = bring(x_ref, xs, x_sem), bring(s_ref, ss, s_sem)
    r_out, d_out = give(pulls, repel_ref, r_sem), give(drives, drive_ref, d_sem)
    get_width = pltpu.make_async_copy(width_hbm, width_ref, own.at[4])
    own_x = pltpu.make_async_copy(x_ref.at[:, columns(g)], xs.at[g], own.at[0])
    own_s = pltpu.make_async_copy(s_ref.at[:, columns(g)], ss.at[g], own.at[1])

    each(1, GROUPS, lambda k: x_in(k).start())
    own_x.start()
    own_s.start()
    get_width.start()
    own_x.wait()
    await_all(xs, GROUPS - 1, x_sem.at[1])
    block = xs[...].reshape(GROUPS * rows, cols)
    inner = lax.dot_general(block, block, (((1,), (1,)), ((), ())), precision=HIGHEST, preferred_element_type=jnp.float32)
    n = GROUPS * rows
    same = lax.broadcasted_iota(jnp.int32, (n, n), 0) == lax.broadcasted_iota(jnp.int32, (n, n), 1)
    norms = jnp.where(same, inner, 0.0)
    part = jnp.sum(norms, axis=1, keepdims=True) + jnp.sum(norms, axis=0, keepdims=True) - 2.0 * inner
    parts[...] = jnp.concatenate([part[: n // 2], part[n // 2 :]], axis=1).reshape(parts.shape)

    def scatter(k):
        q, where = owner_peer(k)
        return pltpu.make_async_remote_copy(
            src_ref=parts.at[q], dst_ref=scattered.at[plane], send_sem=a_sem.at[0], recv_sem=a_sem.at[1],
            device_id=where, device_id_type=MESH)

    def along(k):
        return pltpu.make_async_remote_copy(
            src_ref=lined.at[line], dst_ref=lined.at[line], send_sem=b_sem.at[0], recv_sem=b_sem.at[1],
            device_id=line_peer(k), device_id_type=MESH)

    def gather(k):
        return pltpu.make_async_remote_copy(
            src_ref=gathered.at[owner], dst_ref=gathered.at[owner], send_sem=c_sem.at[0], recv_sem=c_sem.at[1],
            device_id=plane_peer(k)[1], device_id_type=MESH)

    each(OWNERS // 2, OWNERS, lambda k: scatter(k).start())
    each(1 - c, OWNERS // 2, lambda k: scatter(k).start())

    @pl.when(c != 0)
    def _():
        each(1, GROUPS, lambda k: s_in(k).start())


    @pl.when(c == 0)
    def _():
        scattered[plane] = parts[owner]
        await_all(scattered, PLANE - 1, a_sem.at[1])
        lined[line] = jnp.sum(scattered[...], axis=0)
        each(LINE // 2, LINE, lambda k: along(k).start())
        each(1, LINE // 2, lambda k: along(k).start())
        each(1, GROUPS, lambda k: s_in(k).start())
        await_all(lined, LINE - 1, b_sem.at[1])
        gathered[owner] = jnp.sum(lined[...], axis=0)
        each(PLANE // 2, PLANE, lambda k: gather(k).start())
        each(1, PLANE // 2, lambda k: gather(k).start())
        await_all(gathered, OWNERS - 1, c_sem.at[1])

    @pl.when(c != 0)
    def _():
        await_all(gathered, OWNERS, c_sem.at[1])

    get_width.wait()
    width = width_ref[0]
    both = gathered[...].reshape(n // 2, 2 * n)
    dist = jnp.concatenate([both[:, :n], both[:, n:]], axis=0)
    kern = jnp.exp(-dist / (width * P_SIZE))
    weight = jnp.sum(kern, axis=1, keepdims=True)
    block = xs[...].reshape(n, cols)
    pull = jnp.dot(kern, block, precision=HIGHEST, preferred_element_type=jnp.float32)
    pulls[...] = ((block * weight - pull) / (n * width)).reshape(pulls.shape)
    each(1, GROUPS, lambda k: r_out(k).start())
    own_r = pltpu.make_async_copy(pulls.at[g], repel_ref.at[:, columns(g)], own.at[2])
    own_r.start()

    own_s.wait()
    await_all(ss, GROUPS - 1, s_sem.at[1])
    block = ss[...].reshape(n, cols)
    drive = jnp.dot(kern, block, precision=HIGHEST, preferred_element_type=jnp.float32)
    drives[...] = (drive / n).reshape(drives.shape)
    each(1, GROUPS, lambda k: d_out(k).start())
    own_d = pltpu.make_async_copy(drives.at[g], drive_ref.at[:, columns(g)], own.at[3])
    own_d.start()

    await_all(xs, GROUPS - 1, x_sem.at[0])
    await_all(ss, GROUPS - 1, s_sem.at[0])

    @pl.when(c == 0)
    def _():
        await_all(parts, OWNERS - 1, a_sem.at[0])
        await_all(lined, LINE - 1, b_sem.at[0])
        await_all(scattered, PLANE - 1, c_sem.at[0])

    @pl.when(c != 0)
    def _():
        await_all(parts, OWNERS, a_sem.at[0])

    own_r.wait()
    own_d.wait()
    for sem in (r_sem, d_sem):
        await_all(pulls, GROUPS - 1, sem.at[0])
        await_all(pulls, GROUPS - 1, sem.at[1])


def shards(particles, scores, kernel_width):
    rows, length = particles.shape
    cols = length // GROUPS
    n = GROUPS * rows
    whole = pltpu.VMEM((GROUPS, rows, cols), jnp.float32)
    piece = (n * n // (OWNERS * 2 * n), 2 * n)
    out = jax.ShapeDtypeStruct(particles.shape, jnp.float32)
    dma = pltpu.SemaphoreType.DMA
    repel, drive = pl.pallas_call(
        kernel,
        out_shape=(out, out),
        in_specs=[pl.BlockSpec(memory_space=pl.ANY)] * 3,
        out_specs=(pl.BlockSpec(memory_space=pltpu.VMEM),) * 2,
        scratch_shapes=[whole] * 4
        + [pltpu.VMEM((k, *piece), jnp.float32) for k in (OWNERS, PLANE, LINE, OWNERS)]
        + [pltpu.SMEM((1,), jnp.float32), dma((5,))] + [dma((2,))] * 7,
        compiler_params=pltpu.CompilerParams(collective_id=0, has_side_effects=True, vmem_limit_bytes=55050240),
    )(kernel_width, particles, scores)
    return (drive, repel)


def solution(mesh):
    return jax.shard_map(
        shards,
        mesh=mesh,
        in_specs=(P("grp", "par"), P("grp", "par"), P()),
        out_specs=(P("grp", "par"), P("grp", "par")),
        check_vma=False,
    )
```

```python
import jax
import jax.numpy as jnp
from jax import lax
from jax.experimental import pallas as pl
from jax.experimental.pallas import tpu as pltpu
from jax.sharding import PartitionSpec as P

P_SIZE = 1048576
MESH = pl.DeviceIdType.MESH
HIGHEST = lax.Precision.HIGHEST
Y, ZH, ZL, X, C = 4, 4, 4, 4, 2
GROUPS, PLANE, LINE, OWNERS = Y * ZH, Y * X * C, ZH * ZL, Y * X


def turn(a, b, n):
    return lax.rem(a + b, n)


def kernel(width_hbm, x_ref, s_ref, repel_ref, drive_ref, xs, ss, pulls, drives, parts, scattered, lined, gathered,
           width_ref, own, x_sem, r_sem, d_sem, a_sem, b_sem, c_sem, ts, twin_drives, t_sem):
    g, p = lax.axis_index("grp"), lax.axis_index("par")
    y, zh = lax.div(g, ZH), lax.rem(g, ZH)
    zl, x, c = lax.div(p, X * C), lax.rem(lax.div(p, C), X), lax.rem(p, C)
    plane = (y * X + x) * C + c
    owner, line = y * X + x, zh * ZL + zl
    rows, cols = xs.shape[1], xs.shape[2]

    def at(dy, dz):
        return turn(y, dy, Y) * ZH + turn(zh, dz, ZH)

    elder = at(0, ZH - 1)

    def group_peer(k):
        return turn(y, lax.div(k, ZH), Y) * ZH + turn(zh, lax.rem(k, ZH), ZH)

    def plane_peer(k):
        py, px = turn(y, lax.div(k, X * C), Y), turn(x, lax.rem(lax.div(k, C), X), X)
        pc = turn(c, lax.rem(k, C), C)
        return (py * X + px) * C + pc, {"grp": py * ZH + zh, "par": zl * (X * C) + px * C + pc}

    def owner_peer(k):
        py, px = turn(y, lax.div(k, X), Y), turn(x, lax.rem(k, X), X)
        return py * X + px, {"grp": py * ZH + zh, "par": zl * (X * C) + px * C}

    def line_peer(k):
        ph, pz = turn(zh, lax.div(k, ZL), ZH), turn(zl, lax.rem(k, ZL), ZL)
        return {"grp": y * ZH + ph, "par": pz * (X * C) + x * C + c}

    def columns(q):
        return pl.ds(pl.multiple_of(q * cols, cols), cols)

    def each(low, high, body):
        lax.fori_loop(low, high, lambda k, _: (body(k), None)[1], None)

    barrier = pltpu.get_barrier_semaphore()

    def greet(where):
        pl.semaphore_signal(barrier, inc=1, device_id=where, device_id_type=MESH)

    each(1, GROUPS, lambda k: greet({"grp": group_peer(k)}))

    @pl.when(c == 0)
    def _():
        each(1, LINE, lambda k: greet(line_peer(k)))
        each(1, PLANE, lambda k: greet(plane_peer(k)[1]))
        pl.semaphore_wait(barrier, GROUPS + LINE + PLANE - 3)

    @pl.when(c != 0)
    def _():
        each(0, OWNERS, lambda k: greet(owner_peer(k)[1]))
        pl.semaphore_wait(barrier, GROUPS + OWNERS - 1)

    def bring(src, dst, sem):
        def copy(k):
            q = group_peer(k)
            return pltpu.make_async_remote_copy(
                src_ref=src.at[:, columns(q)], dst_ref=dst.at[g], send_sem=sem.at[0], recv_sem=sem.at[1],
                device_id={"grp": q}, device_id_type=MESH)
        return copy

    def give(src, dst, sem):
        def copy(k):
            q = group_peer(k)
            return pltpu.make_async_remote_copy(
                src_ref=src.at[q], dst_ref=dst.at[:, columns(g)], send_sem=sem.at[0], recv_sem=sem.at[1],
                device_id={"grp": q}, device_id_type=MESH)
        return copy

    def await_all(buffer, count, sem):
        whole = buffer.at[pl.ds(0, count)]
        pltpu.make_async_copy(whole, whole, sem).wait()

    x_in, r_out = bring(x_ref, xs, x_sem), give(pulls, repel_ref, r_sem)
    get_width = pltpu.make_async_copy(width_hbm, width_ref, own.at[4])
    own_x = pltpu.make_async_copy(x_ref.at[:, columns(g)], xs.at[g], own.at[0])
    own_s = pltpu.make_async_copy(s_ref.at[:, columns(g)], ss.at[g], own.at[1])

    def send(src, dst, where, send_sem, recv_sem):
        return pltpu.make_async_remote_copy(
            src_ref=src, dst_ref=dst, send_sem=t_sem.at[send_sem], recv_sem=t_sem.at[recv_sem],
            device_id={"grp": where}, device_id_type=MESH)

    def to_owner(dy, dz, recv):
        q = at(dy, dz)
        send(s_ref.at[:, columns(q)], ss.at[g], q, 0, recv).start()

    def to_twin(dy, dz, recv):
        send(s_ref.at[:, columns(at(dy, dz))], ts.at[g], at(dy, dz + 1), 1, recv).start()

    def on_to_twin(dy):
        h = at(dy, ZH - 1)
        send(ss.at[h], ts.at[h], at(0, 1), 2, 7).start()

    def on_to_owner(dy):
        h = at(dy, 1)
        send(ts.at[h], ss.at[h], elder, 2, 8).start()

    own_t = pltpu.make_async_copy(s_ref.at[:, columns(elder)], ts.at[g], own.at[5])
    own_e = pltpu.make_async_copy(twin_drives.at[g], drive_ref.at[:, columns(elder)], own.at[6])

    each(1, GROUPS, lambda k: x_in(k).start())
    own_x.start()
    own_s.start()
    get_width.start()
    own_t.start()

    @pl.when(c != 0)
    def _():
        each(0, Y, lambda k: to_owner(k, 1, 3))
        each(0, Y, lambda k: to_twin(k, 2, 4))


    own_x.wait()
    await_all(xs, GROUPS - 1, x_sem.at[1])
    block = xs[...].reshape(GROUPS * rows, cols)
    inner = lax.dot_general(block, block, (((1,), (1,)), ((), ())), precision=HIGHEST, preferred_element_type=jnp.float32)
    n = GROUPS * rows
    same = lax.broadcasted_iota(jnp.int32, (n, n), 0) == lax.broadcasted_iota(jnp.int32, (n, n), 1)
    norms = jnp.where(same, inner, 0.0)
    part = jnp.sum(norms, axis=1, keepdims=True) + jnp.sum(norms, axis=0, keepdims=True) - 2.0 * inner
    parts[...] = jnp.concatenate([part[: n // 2], part[n // 2 :]], axis=1).reshape(parts.shape)

    def scatter(k):
        q, where = owner_peer(k)
        return pltpu.make_async_remote_copy(
            src_ref=parts.at[q], dst_ref=scattered.at[plane], send_sem=a_sem.at[0], recv_sem=a_sem.at[1],
            device_id=where, device_id_type=MESH)

    def along(k):
        return pltpu.make_async_remote_copy(
            src_ref=lined.at[line], dst_ref=lined.at[line], send_sem=b_sem.at[0], recv_sem=b_sem.at[1],
            device_id=line_peer(k), device_id_type=MESH)

    def gather(k):
        return pltpu.make_async_remote_copy(
            src_ref=gathered.at[owner], dst_ref=gathered.at[owner], send_sem=c_sem.at[0], recv_sem=c_sem.at[1],
            device_id=plane_peer(k)[1], device_id_type=MESH)

    each(OWNERS // 2, OWNERS, lambda k: scatter(k).start())
    each(1 - c, OWNERS // 2, lambda k: scatter(k).start())


    @pl.when(c != 0)
    def _():
        each(0, Y, lambda k: to_owner(k, 3, 5))
        each(0, Y, lambda k: to_twin(k, 0, 6))
        each(1, Y, lambda k: to_owner(k, 0, 5))
        each(1, Y, lambda k: to_twin(k, 3, 6))


    @pl.when(c == 0)
    def _():
        scattered[plane] = parts[owner]
        await_all(scattered, PLANE - 1, a_sem.at[1])
        lined[line] = jnp.sum(scattered[...], axis=0)
        each(LINE // 2, LINE, lambda k: along(k).start())
        each(1, LINE // 2, lambda k: along(k).start())
        each(0, Y, lambda k: to_owner(k, 1, 3))
        each(0, Y, lambda k: to_twin(k, 2, 4))
        each(0, Y, lambda k: to_owner(k, 3, 5))
        each(0, Y, lambda k: to_twin(k, 0, 6))
        each(1, Y, lambda k: to_owner(k, 0, 5))
        each(1, Y, lambda k: to_twin(k, 3, 6))
        await_all(lined, LINE - 1, b_sem.at[1])
        gathered[owner] = jnp.sum(lined[...], axis=0)
        each(PLANE // 2, PLANE, lambda k: gather(k).start())
        each(1, PLANE // 2, lambda k: gather(k).start())
        await_all(ss, Y, t_sem.at[3])
        each(0, Y, on_to_twin)
        await_all(ts, Y, t_sem.at[4])
        each(0, Y, on_to_owner)
        await_all(gathered, OWNERS - 1, c_sem.at[1])

    @pl.when(c != 0)
    def _():
        await_all(ss, Y, t_sem.at[3])
        each(0, Y, on_to_twin)
        await_all(ts, Y, t_sem.at[4])
        each(0, Y, on_to_owner)
        await_all(gathered, OWNERS, c_sem.at[1])

    get_width.wait()
    width = width_ref[0]
    both = gathered[...].reshape(n // 2, 2 * n)
    dist = jnp.concatenate([both[:, :n], both[:, n:]], axis=0)
    kern = jnp.exp(-dist / (width * P_SIZE))
    weight = jnp.sum(kern, axis=1, keepdims=True)
    block = xs[...].reshape(n, cols)
    pull = jnp.dot(kern, block, precision=HIGHEST, preferred_element_type=jnp.float32)
    pulls[...] = ((block * weight - pull) / (n * width)).reshape(pulls.shape)
    each(1, GROUPS, lambda k: r_out(k).start())
    own_r = pltpu.make_async_copy(pulls.at[g], repel_ref.at[:, columns(g)], own.at[2])
    own_r.start()

    own_s.wait()
    await_all(ss, 2 * Y - 1, t_sem.at[5])
    await_all(ss, Y, t_sem.at[8])

    def driven(scores):
        block = scores[...].reshape(n, cols)
        drive = jnp.dot(kern, block, precision=HIGHEST, preferred_element_type=jnp.float32)
        return (drive / n).reshape(drives.shape)

    drives[...] = driven(ss)

    def back(src, piece, dy, dz):
        q = at(dy, dz)
        pltpu.make_async_remote_copy(
            src_ref=src.at[q], dst_ref=drive_ref.at[:, columns(piece)], send_sem=d_sem.at[0], recv_sem=d_sem.at[1],
            device_id={"grp": q}, device_id_type=MESH).start()

    each(0, Y, lambda k: back(drives, g, k, ZH - 1))
    own_t.wait()
    await_all(ts, 2 * Y - 1, t_sem.at[6])
    await_all(ts, Y, t_sem.at[7])
    twin_drives[...] = driven(ts)
    each(0, Y, lambda k: back(twin_drives, elder, k, 1))
    each(1, Y, lambda k: back(drives, g, k, 0))
    each(1, Y, lambda k: back(twin_drives, elder, k, 0))
    own_e.start()
    own_d = pltpu.make_async_copy(drives.at[g], drive_ref.at[:, columns(g)], own.at[3])
    own_d.start()

    await_all(xs, GROUPS - 1, x_sem.at[0])
    own_r.wait()
    own_d.wait()

    own_e.wait()
    await_all(ss, 3 * Y - 1, t_sem.at[0])
    await_all(ts, 3 * Y - 1, t_sem.at[1])
    await_all(ss, 2 * Y, t_sem.at[2])
    await_all(pulls, GROUPS - 2, d_sem.at[0])
    await_all(pulls, GROUPS - 2, d_sem.at[1])

    @pl.when(c == 0)
    def _():
        await_all(parts, OWNERS - 1, a_sem.at[0])
        await_all(lined, LINE - 1, b_sem.at[0])
        await_all(scattered, PLANE - 1, c_sem.at[0])

    @pl.when(c != 0)
    def _():
        await_all(parts, OWNERS, a_sem.at[0])

    await_all(pulls, GROUPS - 1, r_sem.at[0])
    await_all(pulls, GROUPS - 1, r_sem.at[1])


def shards(particles, scores, kernel_width):
    rows, length = particles.shape
    cols = length // GROUPS
    n = GROUPS * rows
    whole = pltpu.VMEM((GROUPS, rows, cols), jnp.float32)
    piece = (n * n // (OWNERS * 2 * n), 2 * n)
    out = jax.ShapeDtypeStruct(particles.shape, jnp.float32)
    dma = pltpu.SemaphoreType.DMA
    repel, drive = pl.pallas_call(
        kernel,
        out_shape=(out, out),
        in_specs=[pl.BlockSpec(memory_space=pl.ANY)] * 3,
        out_specs=(pl.BlockSpec(memory_space=pltpu.VMEM),) * 2,
        scratch_shapes=[whole] * 4
        + [pltpu.VMEM((k, *piece), jnp.float32) for k in (OWNERS, PLANE, LINE, OWNERS)]
        + [pltpu.SMEM((1,), jnp.float32), dma((7,))] + [dma((2,))] * 6 + [whole] * 2 + [dma((9,))],
        compiler_params=pltpu.CompilerParams(collective_id=0, has_side_effects=True, vmem_limit_bytes=55050240),
    )(kernel_width, particles, scores)
    return (drive, repel)


def solution(mesh):
    return jax.shard_map(
        shards,
        mesh=mesh,
        in_specs=(P("grp", "par"), P("grp", "par"), P()),
        out_specs=(P("grp", "par"), P("grp", "par")),
        check_vma=False,
    )
```

```python
import jax
import jax.numpy as jnp
from jax import lax
from jax.experimental import pallas as pl
from jax.experimental.pallas import tpu as pltpu
from jax.sharding import PartitionSpec as P

P_SIZE = 1048576
MESH = pl.DeviceIdType.MESH
HIGHEST = lax.Precision.HIGHEST
Y, ZH, ZL, X, C = 4, 4, 4, 4, 2
GROUPS, PLANE, LINE, OWNERS = Y * ZH, Y * X * C, ZH * ZL, Y * X


def turn(a, b, n):
    return lax.rem(a + b, n)


def kernel(width_hbm, x_ref, s_ref, repel_ref, drive_ref, xs, ss, pulls, drives, parts, scattered, lined, gathered,
           width_ref, own, x_sem, r_sem, d_sem, a_sem, b_sem, c_sem, ts, twin_drives, t_sem):
    g, p = lax.axis_index("grp"), lax.axis_index("par")
    y, zh = lax.div(g, ZH), lax.rem(g, ZH)
    zl, x, c = lax.div(p, X * C), lax.rem(lax.div(p, C), X), lax.rem(p, C)
    plane = (y * X + x) * C + c
    owner, line = y * X + x, zh * ZL + zl
    rows, cols = xs.shape[1], xs.shape[2]

    def at(dy, dz):
        return turn(y, dy, Y) * ZH + turn(zh, dz, ZH)

    elder = at(0, ZH - 1)

    def group_peer(k):
        return turn(y, lax.div(k, ZH), Y) * ZH + turn(zh, lax.rem(k, ZH), ZH)

    def plane_peer(k):
        py, px = turn(y, lax.div(k, X * C), Y), turn(x, lax.rem(lax.div(k, C), X), X)
        pc = turn(c, lax.rem(k, C), C)
        return (py * X + px) * C + pc, {"grp": py * ZH + zh, "par": zl * (X * C) + px * C + pc}

    def owner_peer(k):
        py, px = turn(y, lax.div(k, X), Y), turn(x, lax.rem(k, X), X)
        return py * X + px, {"grp": py * ZH + zh, "par": zl * (X * C) + px * C}

    def line_peer(k):
        ph, pz = turn(zh, lax.div(k, ZL), ZH), turn(zl, lax.rem(k, ZL), ZL)
        return {"grp": y * ZH + ph, "par": pz * (X * C) + x * C + c}

    def columns(q):
        return pl.ds(pl.multiple_of(q * cols, cols), cols)

    def each(low, high, body):
        lax.fori_loop(low, high, lambda k, _: (body(k), None)[1], None)

    barrier = pltpu.get_barrier_semaphore()

    def greet(where):
        pl.semaphore_signal(barrier, inc=1, device_id=where, device_id_type=MESH)

    each(1, GROUPS, lambda k: greet({"grp": group_peer(k)}))

    @pl.when(c == 0)
    def _():
        each(1, LINE, lambda k: greet(line_peer(k)))
        each(1, PLANE, lambda k: greet(plane_peer(k)[1]))
        pl.semaphore_wait(barrier, GROUPS + LINE + PLANE - 3)

    @pl.when(c != 0)
    def _():
        each(0, OWNERS, lambda k: greet(owner_peer(k)[1]))
        pl.semaphore_wait(barrier, GROUPS + OWNERS - 1)

    def bring(src, dst, sem):
        def copy(k):
            q = group_peer(k)
            return pltpu.make_async_remote_copy(
                src_ref=src.at[:, columns(q)], dst_ref=dst.at[g], send_sem=sem.at[0], recv_sem=sem.at[1],
                device_id={"grp": q}, device_id_type=MESH)
        return copy

    def give(src, dst, sem):
        def copy(k):
            q = group_peer(k)
            return pltpu.make_async_remote_copy(
                src_ref=src.at[q], dst_ref=dst.at[:, columns(g)], send_sem=sem.at[0], recv_sem=sem.at[1],
                device_id={"grp": q}, device_id_type=MESH)
        return copy

    def await_all(buffer, count, sem):
        whole = buffer.at[pl.ds(0, count)]
        pltpu.make_async_copy(whole, whole, sem).wait()

    x_in, r_out = bring(x_ref, xs, x_sem), give(pulls, repel_ref, r_sem)
    get_width = pltpu.make_async_copy(width_hbm, width_ref, own.at[4])
    own_x = pltpu.make_async_copy(x_ref.at[:, columns(g)], xs.at[g], own.at[0])
    own_s = pltpu.make_async_copy(s_ref.at[:, columns(g)], ss.at[g], own.at[1])

    def send(src, dst, where, send_sem, recv_sem):
        return pltpu.make_async_remote_copy(
            src_ref=src, dst_ref=dst, send_sem=t_sem.at[send_sem], recv_sem=t_sem.at[recv_sem],
            device_id={"grp": where}, device_id_type=MESH)

    def to_owner(dy, dz, recv):
        q = at(dy, dz)
        send(s_ref.at[:, columns(q)], ss.at[g], q, 0, recv).start()

    def to_twin(dy, dz, recv):
        send(s_ref.at[:, columns(at(dy, dz))], ts.at[g], at(dy, dz + 1), 1, recv).start()

    def on_to_twin(dy):
        h = at(dy, ZH - 1)
        send(ss.at[h], ts.at[h], at(0, 1), 2, 7).start()

    def on_to_owner(dy):
        h = at(dy, 1)
        send(ts.at[h], ss.at[h], elder, 2, 8).start()

    own_t = pltpu.make_async_copy(s_ref.at[:, columns(elder)], ts.at[g], own.at[5])
    own_e = pltpu.make_async_copy(twin_drives.at[g], drive_ref.at[:, columns(elder)], own.at[6])

    each(1, GROUPS, lambda k: x_in(k).start())
    own_x.start()
    own_s.start()
    get_width.start()
    own_t.start()

    @pl.when(c != 0)
    def _():
        each(0, Y, lambda k: to_owner(k, 1, 3))
        each(0, Y, lambda k: to_twin(k, 2, 4))


    own_x.wait()
    await_all(xs, GROUPS - 1, x_sem.at[1])
    block = xs[...].reshape(GROUPS * rows, cols)
    inner = lax.dot_general(block, block, (((1,), (1,)), ((), ())), precision=HIGHEST, preferred_element_type=jnp.float32)
    n = GROUPS * rows
    same = lax.broadcasted_iota(jnp.int32, (n, n), 0) == lax.broadcasted_iota(jnp.int32, (n, n), 1)
    norms = jnp.where(same, inner, 0.0)
    part = jnp.sum(norms, axis=1, keepdims=True) + jnp.sum(norms, axis=0, keepdims=True) - 2.0 * inner
    parts[...] = jnp.concatenate([part[: n // 2], part[n // 2 :]], axis=1).reshape(parts.shape)

    def scatter(k):
        q, where = owner_peer(k)
        return pltpu.make_async_remote_copy(
            src_ref=parts.at[q], dst_ref=scattered.at[plane], send_sem=a_sem.at[0], recv_sem=a_sem.at[1],
            device_id=where, device_id_type=MESH)

    def along(k):
        return pltpu.make_async_remote_copy(
            src_ref=lined.at[line], dst_ref=lined.at[line], send_sem=b_sem.at[0], recv_sem=b_sem.at[1],
            device_id=line_peer(k), device_id_type=MESH)

    def gather(k):
        return pltpu.make_async_remote_copy(
            src_ref=gathered.at[owner], dst_ref=gathered.at[owner], send_sem=c_sem.at[0], recv_sem=c_sem.at[1],
            device_id=plane_peer(k)[1], device_id_type=MESH)

    each(OWNERS // 2, OWNERS, lambda k: scatter(k).start())
    each(1 - c, OWNERS // 2, lambda k: scatter(k).start())


    @pl.when(c != 0)
    def _():
        each(0, Y, lambda k: to_owner(k, 3, 5))
        each(0, Y, lambda k: to_twin(k, 0, 6))
        each(1, Y, lambda k: to_owner(k, 0, 5))
        each(1, Y, lambda k: to_twin(k, 3, 6))


    @pl.when(c == 0)
    def _():
        scattered[plane] = parts[owner]
        await_all(scattered, PLANE - 1, a_sem.at[1])
        lined[line] = jnp.sum(scattered[...], axis=0)
        each(LINE // 2, LINE, lambda k: along(k).start())
        each(1, LINE // 2, lambda k: along(k).start())
        each(0, Y, lambda k: to_owner(k, 1, 3))
        each(0, Y, lambda k: to_twin(k, 2, 4))
        each(0, Y, lambda k: to_owner(k, 3, 5))
        each(0, Y, lambda k: to_twin(k, 0, 6))
        each(1, Y, lambda k: to_owner(k, 0, 5))
        each(1, Y, lambda k: to_twin(k, 3, 6))
        await_all(lined, LINE - 1, b_sem.at[1])
        gathered[owner] = jnp.sum(lined[...], axis=0)
        each(PLANE // 2, PLANE, lambda k: gather(k).start())
        each(1, PLANE // 2, lambda k: gather(k).start())
        await_all(ss, Y, t_sem.at[3])
        each(0, Y, on_to_twin)
        await_all(ts, Y, t_sem.at[4])
        each(0, Y, on_to_owner)
        await_all(gathered, OWNERS - 1, c_sem.at[1])

    @pl.when(c != 0)
    def _():
        await_all(ss, Y, t_sem.at[3])
        each(0, Y, on_to_twin)
        await_all(ts, Y, t_sem.at[4])
        each(0, Y, on_to_owner)
        await_all(gathered, OWNERS, c_sem.at[1])

    get_width.wait()
    width = width_ref[0]
    both = gathered[...].reshape(n // 2, 2 * n)
    dist = jnp.concatenate([both[:, :n], both[:, n:]], axis=0)
    kern = jnp.exp(-dist / (width * P_SIZE))
    weight = jnp.sum(kern, axis=1, keepdims=True)
    block = xs[...].reshape(n, cols)
    pull = jnp.dot(kern, block, precision=HIGHEST, preferred_element_type=jnp.float32)
    pulls[...] = ((block * weight - pull) / width).reshape(pulls.shape)
    each(1, GROUPS, lambda k: r_out(k).start())
    own_r = pltpu.make_async_copy(pulls.at[g], repel_ref.at[:, columns(g)], own.at[2])
    own_r.start()

    own_s.wait()
    await_all(ss, 2 * Y - 1, t_sem.at[5])
    await_all(ss, Y, t_sem.at[8])

    def driven(scores):
        block = scores[...].reshape(n, cols)
        drive = jnp.dot(kern, block, precision=HIGHEST, preferred_element_type=jnp.float32)
        return drive.reshape(drives.shape)

    drives[...] = driven(ss)

    def back(src, piece, dy, dz):
        q = at(dy, dz)
        pltpu.make_async_remote_copy(
            src_ref=src.at[q], dst_ref=drive_ref.at[:, columns(piece)], send_sem=d_sem.at[0], recv_sem=d_sem.at[1],
            device_id={"grp": q}, device_id_type=MESH).start()

    each(0, Y, lambda k: back(drives, g, k, ZH - 1))
    own_t.wait()
    await_all(ts, 2 * Y - 1, t_sem.at[6])
    await_all(ts, Y, t_sem.at[7])
    twin_drives[...] = driven(ts)
    each(0, Y, lambda k: back(twin_drives, elder, k, 1))
    each(1, Y, lambda k: back(drives, g, k, 0))
    each(1, Y, lambda k: back(twin_drives, elder, k, 0))
    own_e.start()
    own_d = pltpu.make_async_copy(drives.at[g], drive_ref.at[:, columns(g)], own.at[3])
    own_d.start()

    await_all(xs, GROUPS - 1, x_sem.at[0])
    own_r.wait()
    own_d.wait()

    own_e.wait()
    await_all(ss, 3 * Y - 1, t_sem.at[0])
    await_all(ts, 3 * Y - 1, t_sem.at[1])
    await_all(ss, 2 * Y, t_sem.at[2])
    await_all(pulls, GROUPS - 2, d_sem.at[0])
    await_all(pulls, GROUPS - 2, d_sem.at[1])

    @pl.when(c == 0)
    def _():
        await_all(parts, OWNERS - 1, a_sem.at[0])
        await_all(lined, LINE - 1, b_sem.at[0])
        await_all(scattered, PLANE - 1, c_sem.at[0])

    @pl.when(c != 0)
    def _():
        await_all(parts, OWNERS, a_sem.at[0])

    await_all(pulls, GROUPS - 1, r_sem.at[0])
    await_all(pulls, GROUPS - 1, r_sem.at[1])


def shards(particles, scores, kernel_width):
    rows, length = particles.shape
    cols = length // GROUPS
    n = GROUPS * rows
    whole = pltpu.VMEM((GROUPS, rows, cols), jnp.float32)
    piece = (n * n // (OWNERS * 2 * n), 2 * n)
    out = jax.ShapeDtypeStruct(particles.shape, jnp.float32)
    dma = pltpu.SemaphoreType.DMA
    repel, drive = pl.pallas_call(
        kernel,
        out_shape=(out, out),
        in_specs=[pl.BlockSpec(memory_space=pl.ANY)] * 3,
        out_specs=(pl.BlockSpec(memory_space=pltpu.VMEM),) * 2,
        scratch_shapes=[whole] * 4
        + [pltpu.VMEM((k, *piece), jnp.float32) for k in (OWNERS, PLANE, LINE, OWNERS)]
        + [pltpu.SMEM((1,), jnp.float32), dma((7,))] + [dma((2,))] * 6 + [whole] * 2 + [dma((9,))],
        compiler_params=pltpu.CompilerParams(collective_id=0, has_side_effects=True, vmem_limit_bytes=55050240),
    )(kernel_width, particles, scores)
    return (drive / n, repel / n)


def solution(mesh):
    return jax.shard_map(
        shards,
        mesh=mesh,
        in_specs=(P("grp", "par"), P("grp", "par"), P()),
        out_specs=(P("grp", "par"), P("grp", "par")),
        check_vma=False,
    )
```

```python
import jax
import jax.numpy as jnp
from jax import lax
from jax.experimental import pallas as pl
from jax.experimental.pallas import tpu as pltpu
from jax.sharding import PartitionSpec as P

P_SIZE = 1048576
MESH = pl.DeviceIdType.MESH
HIGHEST = lax.Precision.HIGHEST
Y, ZH, ZL, X, C = 4, 4, 4, 4, 2
GROUPS, PLANE, LINE, OWNERS = Y * ZH, Y * X * C, ZH * ZL, Y * X


def turn(a, b, n):
    return lax.rem(a + b, n)


def kernel(width_hbm, x_ref, s_ref, repel_ref, drive_ref, xs, ss, pulls, drives, parts, scattered, lined, gathered,
           width_ref, own, x_sem, r_sem, d_sem, a_sem, b_sem, c_sem, ts, twin_drives, t_sem):
    g, p = lax.axis_index("grp"), lax.axis_index("par")
    y, zh = lax.div(g, ZH), lax.rem(g, ZH)
    zl, x, c = lax.div(p, X * C), lax.rem(lax.div(p, C), X), lax.rem(p, C)
    plane = (y * X + x) * C + c
    owner, line = y * X + x, zh * ZL + zl
    rows, cols = xs.shape[1], xs.shape[2]

    def at(dy, dz):
        return turn(y, dy, Y) * ZH + turn(zh, dz, ZH)

    elder = at(0, ZH - 1)

    def group_peer(k):
        return turn(y, lax.div(k, ZH), Y) * ZH + turn(zh, lax.rem(k, ZH), ZH)

    def plane_peer(k):
        py, px = turn(y, lax.div(k, X * C), Y), turn(x, lax.rem(lax.div(k, C), X), X)
        pc = turn(c, lax.rem(k, C), C)
        return (py * X + px) * C + pc, {"grp": py * ZH + zh, "par": zl * (X * C) + px * C + pc}

    def owner_peer(k):
        py, px = turn(y, lax.div(k, X), Y), turn(x, lax.rem(k, X), X)
        return py * X + px, {"grp": py * ZH + zh, "par": zl * (X * C) + px * C}

    def line_peer(k):
        ph, pz = turn(zh, lax.div(k, ZL), ZH), turn(zl, lax.rem(k, ZL), ZL)
        return {"grp": y * ZH + ph, "par": pz * (X * C) + x * C + c}

    def columns(q):
        return pl.ds(pl.multiple_of(q * cols, cols), cols)

    def each(low, high, body):
        lax.fori_loop(low, high, lambda k, _: (body(k), None)[1], None)

    barrier = pltpu.get_barrier_semaphore()

    def greet(where):
        pl.semaphore_signal(barrier, inc=1, device_id=where, device_id_type=MESH)

    each(1, GROUPS, lambda k: greet({"grp": group_peer(k)}))

    @pl.when(c == 0)
    def _():
        each(1, LINE, lambda k: greet(line_peer(k)))
        each(1, PLANE, lambda k: greet(plane_peer(k)[1]))
        pl.semaphore_wait(barrier, GROUPS + LINE + PLANE - 3)

    @pl.when(c != 0)
    def _():
        each(0, OWNERS, lambda k: greet(owner_peer(k)[1]))
        pl.semaphore_wait(barrier, GROUPS + OWNERS - 1)

    def bring(src, dst, sem):
        def copy(k):
            q = group_peer(k)
            return pltpu.make_async_remote_copy(
                src_ref=src.at[:, columns(q)], dst_ref=dst.at[g], send_sem=sem.at[0], recv_sem=sem.at[1],
                device_id={"grp": q}, device_id_type=MESH)
        return copy

    def give(src, dst, sem):
        def copy(k):
            q = group_peer(k)
            return pltpu.make_async_remote_copy(
                src_ref=src.at[q], dst_ref=dst.at[:, columns(g)], send_sem=sem.at[0], recv_sem=sem.at[1],
                device_id={"grp": q}, device_id_type=MESH)
        return copy

    def await_all(buffer, count, sem):
        whole = buffer.at[pl.ds(0, count)]
        pltpu.make_async_copy(whole, whole, sem).wait()

    x_in, r_out = bring(x_ref, xs, x_sem), give(pulls, repel_ref, r_sem)
    get_width = pltpu.make_async_copy(width_hbm, width_ref, own.at[4])
    own_x = pltpu.make_async_copy(x_ref.at[:, columns(g)], xs.at[g], own.at[0])
    own_s = pltpu.make_async_copy(s_ref.at[:, columns(g)], ss.at[g], own.at[1])

    def send(src, dst, where, send_sem, recv_sem):
        return pltpu.make_async_remote_copy(
            src_ref=src, dst_ref=dst, send_sem=t_sem.at[send_sem], recv_sem=t_sem.at[recv_sem],
            device_id={"grp": where}, device_id_type=MESH)

    def to_owner(dy, dz, recv):
        q = at(dy, dz)
        send(s_ref.at[:, columns(q)], ss.at[g], q, 0, recv).start()

    def to_twin(dy, dz, recv):
        send(s_ref.at[:, columns(at(dy, dz))], ts.at[g], at(dy, dz + 1), 1, recv).start()

    def on_to_twin(dy):
        h = at(dy, ZH - 1)
        send(ss.at[h], ts.at[h], at(0, 1), 2, 7).start()

    def on_to_owner(dy):
        h = at(dy, 1)
        send(ts.at[h], ss.at[h], elder, 2, 8).start()

    own_t = pltpu.make_async_copy(s_ref.at[:, columns(elder)], ts.at[g], own.at[5])
    own_e = pltpu.make_async_copy(twin_drives.at[g], drive_ref.at[:, columns(elder)], own.at[6])

    each(1, GROUPS, lambda k: x_in(k).start())
    own_x.start()
    own_s.start()
    get_width.start()
    own_t.start()
    each(1, Y, lambda k: to_owner(k, 0, 5))
    each(1, Y, lambda k: to_twin(k, 3, 6))

    @pl.when(c != 0)
    def _():
        each(0, Y, lambda k: to_owner(k, 1, 3))
        each(0, Y, lambda k: to_twin(k, 2, 4))


    own_x.wait()
    await_all(xs, GROUPS - 1, x_sem.at[1])
    block = xs[...].reshape(GROUPS * rows, cols)
    inner = lax.dot_general(block, block, (((1,), (1,)), ((), ())), precision=HIGHEST, preferred_element_type=jnp.float32)
    n = GROUPS * rows
    same = lax.broadcasted_iota(jnp.int32, (n, n), 0) == lax.broadcasted_iota(jnp.int32, (n, n), 1)
    norms = jnp.where(same, inner, 0.0)
    part = jnp.sum(norms, axis=1, keepdims=True) + jnp.sum(norms, axis=0, keepdims=True) - 2.0 * inner
    parts[...] = jnp.concatenate([part[: n // 2], part[n // 2 :]], axis=1).reshape(parts.shape)

    def scatter(k):
        q, where = owner_peer(k)
        return pltpu.make_async_remote_copy(
            src_ref=parts.at[q], dst_ref=scattered.at[plane], send_sem=a_sem.at[0], recv_sem=a_sem.at[1],
            device_id=where, device_id_type=MESH)

    def along(k):
        return pltpu.make_async_remote_copy(
            src_ref=lined.at[line], dst_ref=lined.at[line], send_sem=b_sem.at[0], recv_sem=b_sem.at[1],
            device_id=line_peer(k), device_id_type=MESH)

    def gather(k):
        return pltpu.make_async_remote_copy(
            src_ref=gathered.at[owner], dst_ref=gathered.at[owner], send_sem=c_sem.at[0], recv_sem=c_sem.at[1],
            device_id=plane_peer(k)[1], device_id_type=MESH)

    each(OWNERS // 2, OWNERS, lambda k: scatter(k).start())
    each(1 - c, OWNERS // 2, lambda k: scatter(k).start())


    @pl.when(c != 0)
    def _():
        each(0, Y, lambda k: to_owner(k, 3, 5))
        each(0, Y, lambda k: to_twin(k, 0, 6))


    @pl.when(c == 0)
    def _():
        scattered[plane] = parts[owner]
        await_all(scattered, PLANE - 1, a_sem.at[1])
        lined[line] = jnp.sum(scattered[...], axis=0)
        each(LINE // 2, LINE, lambda k: along(k).start())
        each(1, LINE // 2, lambda k: along(k).start())
        each(0, Y, lambda k: to_owner(k, 1, 3))
        each(0, Y, lambda k: to_twin(k, 2, 4))
        each(0, Y, lambda k: to_owner(k, 3, 5))
        each(0, Y, lambda k: to_twin(k, 0, 6))
        await_all(lined, LINE - 1, b_sem.at[1])
        gathered[owner] = jnp.sum(lined[...], axis=0)
        each(PLANE // 2, PLANE, lambda k: gather(k).start())
        each(1, PLANE // 2, lambda k: gather(k).start())
        await_all(ss, Y, t_sem.at[3])
        each(0, Y, on_to_twin)
        await_all(ts, Y, t_sem.at[4])
        each(0, Y, on_to_owner)
        await_all(gathered, OWNERS - 1, c_sem.at[1])

    @pl.when(c != 0)
    def _():
        await_all(ss, Y, t_sem.at[3])
        each(0, Y, on_to_twin)
        await_all(ts, Y, t_sem.at[4])
        each(0, Y, on_to_owner)
        await_all(gathered, OWNERS, c_sem.at[1])

    get_width.wait()
    width = width_ref[0]
    both = gathered[...].reshape(n // 2, 2 * n)
    dist = jnp.concatenate([both[:, :n], both[:, n:]], axis=0)
    kern = jnp.exp(-dist / (width * P_SIZE))
    weight = jnp.sum(kern, axis=1, keepdims=True)
    block = xs[...].reshape(n, cols)
    pull = jnp.dot(kern, block, precision=HIGHEST, preferred_element_type=jnp.float32)
    pulls[...] = ((block * weight - pull) / width).reshape(pulls.shape)
    each(1, GROUPS, lambda k: r_out(k).start())
    own_r = pltpu.make_async_copy(pulls.at[g], repel_ref.at[:, columns(g)], own.at[2])
    own_r.start()

    own_s.wait()
    await_all(ss, 2 * Y - 1, t_sem.at[5])
    await_all(ss, Y, t_sem.at[8])

    def driven(scores):
        block = scores[...].reshape(n, cols)
        drive = jnp.dot(kern, block, precision=HIGHEST, preferred_element_type=jnp.float32)
        return drive.reshape(drives.shape)

    drives[...] = driven(ss)

    def back(src, piece, dy, dz):
        q = at(dy, dz)
        pltpu.make_async_remote_copy(
            src_ref=src.at[q], dst_ref=drive_ref.at[:, columns(piece)], send_sem=d_sem.at[0], recv_sem=d_sem.at[1],
            device_id={"grp": q}, device_id_type=MESH).start()

    each(0, Y, lambda k: back(drives, g, k, ZH - 1))
    own_t.wait()
    await_all(ts, 2 * Y - 1, t_sem.at[6])
    await_all(ts, Y, t_sem.at[7])
    twin_drives[...] = driven(ts)
    each(0, Y, lambda k: back(twin_drives, elder, k, 1))
    each(1, Y, lambda k: back(drives, g, k, 0))
    each(1, Y, lambda k: back(twin_drives, elder, k, 0))
    own_e.start()
    own_d = pltpu.make_async_copy(drives.at[g], drive_ref.at[:, columns(g)], own.at[3])
    own_d.start()

    await_all(xs, GROUPS - 1, x_sem.at[0])
    own_r.wait()
    own_d.wait()

    own_e.wait()
    await_all(ss, 3 * Y - 1, t_sem.at[0])
    await_all(ts, 3 * Y - 1, t_sem.at[1])
    await_all(ss, 2 * Y, t_sem.at[2])
    await_all(pulls, GROUPS - 2, d_sem.at[0])
    await_all(pulls, GROUPS - 2, d_sem.at[1])

    @pl.when(c == 0)
    def _():
        await_all(parts, OWNERS - 1, a_sem.at[0])
        await_all(lined, LINE - 1, b_sem.at[0])
        await_all(scattered, PLANE - 1, c_sem.at[0])

    @pl.when(c != 0)
    def _():
        await_all(parts, OWNERS, a_sem.at[0])

    await_all(pulls, GROUPS - 1, r_sem.at[0])
    await_all(pulls, GROUPS - 1, r_sem.at[1])


def shards(particles, scores, kernel_width):
    rows, length = particles.shape
    cols = length // GROUPS
    n = GROUPS * rows
    whole = pltpu.VMEM((GROUPS, rows, cols), jnp.float32)
    piece = (n * n // (OWNERS * 2 * n), 2 * n)
    out = jax.ShapeDtypeStruct(particles.shape, jnp.float32)
    dma = pltpu.SemaphoreType.DMA
    repel, drive = pl.pallas_call(
        kernel,
        out_shape=(out, out),
        in_specs=[pl.BlockSpec(memory_space=pl.ANY)] * 3,
        out_specs=(pl.BlockSpec(memory_space=pltpu.VMEM),) * 2,
        scratch_shapes=[whole] * 4
        + [pltpu.VMEM((k, *piece), jnp.float32) for k in (OWNERS, PLANE, LINE, OWNERS)]
        + [pltpu.SMEM((1,), jnp.float32), dma((7,))] + [dma((2,))] * 6 + [whole] * 2 + [dma((9,))],
        compiler_params=pltpu.CompilerParams(collective_id=0, has_side_effects=True, vmem_limit_bytes=55050240),
    )(kernel_width, particles, scores)
    return (drive / n, repel / n)


def solution(mesh):
    return jax.shard_map(
        shards,
        mesh=mesh,
        in_specs=(P("grp", "par"), P("grp", "par"), P()),
        out_specs=(P("grp", "par"), P("grp", "par")),
        check_vma=False,
    )
```
